32 devices in a mesh: groups: 2 (over y), pool: 8 (over z, x), tp: 2 (over core).
Axes of the slice: x: 2, y: 2, z: 4, core: 2. Of those that a mesh axis runs over, the one named last changes fastest.
Arguments:
- prompt_states: bfloat16 [1024, 7168], P(('groups', 'pool'), 'tp'), parts along dimension 0, may hold values from -6 to 6
- down_kv: bfloat16 [7168, 576], P('tp'), may hold values from -0.0625 to 0.0625
- kv_gain: float32 [512], replicated, may hold values from 0.1 to 1.9
- queries: bfloat16 [64, 128, 576], P(('groups', 'pool'), 'tp'), parts along dimension 0, may hold values from -110 to 110
- row_prompt: int32 [64], P(('groups', 'pool')), parts along dimension 0, may hold values from 0 to 3, as said below
- prompt_len: int32 [8], P('groups'), parts along dimension 0, may hold values from 1 to 128, as said below
Outputs:
- attended: bfloat16 [64, 128, 512], P(('groups', 'pool'), 'tp'), parts along dimension 0
The draws below stay inside these ranges and needn't reach their ends.
There are 2 independent parts, one for each index of `groups`. The reference program is written for one: setup_inputs(seed, part) draws one part's arguments, and reference() takes and returns one part's arrays. A program takes and returns all parts, laid end to end along the dimension named above; an argument that names none is the same for every part. Nothing has to cross between parts.
Inputs may be any that keep to these rules, and one draw needn't show every extreme that they name: `row_prompt`: the rows fall in 4 aligned blocks of 8 rows; every row of block b continues prompt b XOR s, with one s of 0 to 3 for the whole draw. `prompt_len`: some prompt has all 128 tokens.
All inputs are finite; a program needn't handle non-finite values.
Results may differ from the reference program's by a relative error of at most 0.0045.
The reference program's roundings to bfloat16 on the way (of `kv_cache` and `weights`) count: a program that leaves them out, or rounds other values in their place, can miss the bound.
Values may be sent and summed in bfloat16 or wider, within the bound.
No kernel may reach another device: no remote copies, remote signals or barrier semaphores. Data moves between devices by JAX's collectives and lax.ppermute only.
A program may use at most 64 MiB of HBM per device.

```python
import jax
import jax.numpy as jnp
from jax import lax

D = 7168
HEADS = 128
KV_RANK = 512
LATENT = 576
PROMPTS = 4
TOKENS = 512
LEN = 128
ROWS = 32


def draw_queries(key, part):
    key = jax.random.fold_in(key, 11)
    values = jnp.clip(jax.random.normal(key, (ROWS, HEADS, LATENT), jnp.float32), -6.0, 6.0)
    return values.astype(jnp.bfloat16)


def draw_row_prompt(key, part):
    key = jax.random.fold_in(key, 7)
    offset = jax.random.randint(key, (), 0, PROMPTS)
    block = jnp.arange(ROWS, dtype=jnp.int32) // (ROWS // PROMPTS)
    return jnp.bitwise_xor(block, offset).astype(jnp.int32)


def draw_prompt_len(key, part):
    key = jax.random.fold_in(key, 3)
    length_key, pick_key = jax.random.split(key)
    lengths = jax.random.randint(length_key, (PROMPTS,), 1, LEN + 1)
    longest = jax.random.randint(pick_key, (), 0, PROMPTS)
    return jnp.where(jnp.arange(PROMPTS) == longest, LEN, lengths).astype(jnp.int32)


def levels(key, shape, shards, low, top_value):
    level = 1.0
    for position, blocks in shards:
        draws = jax.random.uniform(jax.random.fold_in(jax.random.fold_in(key, 6), position), (blocks,), jnp.float32, low / len(shards), top_value / len(shards))
        level = level * jnp.repeat(jnp.exp(draws), shape[position] // blocks).reshape((-1,) + (1,) * (len(shape) - 1 - position))
    return level


def noise(key, dims, scale, reach, shards=(), held_as=jnp.bfloat16):
    entries = jax.random.normal(key, dims, jnp.float32) * scale
    if len(shards) > 0:
        entries = levels(key, dims, shards, -0.22, 0.18) * entries
    return jnp.clip(entries, min=-reach, max=reach).astype(held_as)


def setup_inputs(seed: int = 0, part: int = 0) -> dict:
    streams_of = jax.random.split(jax.random.key(seed), 7)
    own_keys = jax.random.split(jax.random.fold_in(streams_of[6], part), 7)
    return {
        "prompt_states": noise(own_keys[0], (TOKENS, D), 1.0, 6.0, ((0, 8), (1, 2))),
        "down_kv": noise(streams_of[1], (D, LATENT), D ** -0.5, 0.0625, ((0, 2),)),
        "kv_gain": jnp.clip(1.0 + 0.18 * jax.random.normal(streams_of[2], (KV_RANK,), jnp.float32), 0.1, 1.9),
        "queries": draw_queries(jax.random.fold_in(jax.random.fold_in(streams_of[6], part), 71), part),
        "row_prompt": draw_row_prompt(jax.random.fold_in(jax.random.fold_in(streams_of[6], part), 71), part),
        "prompt_len": draw_prompt_len(jax.random.fold_in(jax.random.fold_in(streams_of[6], part), 71), part),
    }


score_scale = 192.0 ** (-0.5)

def rotate(rotary_part, positions):
    half_width = rotary_part.shape[1] // 2
    inverse = 10000.0 ** (-(jnp.arange(half_width, dtype=jnp.float32) * 2.0) / rotary_part.shape[1])
    angles = positions.astype(jnp.float32)[:, None] * inverse[None, :]
    front_half = rotary_part[:, :half_width]
    back_half = rotary_part[:, half_width:]
    cosine = jnp.cos(angles)
    sine = jnp.sin(angles)
    return jnp.concatenate([front_half * cosine - back_half * sine, back_half * cosine + front_half * sine], axis=1)

def encode(projected, kv_gain, positions):
    content = projected[:, :KV_RANK]
    normed = content * lax.rsqrt(lax.optimization_barrier(jnp.mean(content * content, axis=1, keepdims=True)) + 1e-06) * kv_gain
    return jnp.concatenate([normed, rotate(projected[:, KV_RANK:], positions)], axis=1).astype(jnp.bfloat16)

def reference(prompt_states, down_kv, kv_gain, queries, row_prompt, prompt_len):
    projected = jnp.dot(prompt_states, down_kv, preferred_element_type=jnp.float32)
    positions = jnp.arange(TOKENS, dtype=jnp.int32) % LEN
    kv_cache = encode(projected, kv_gain, positions)

    def one_row(inputs):
        query_row, prompt = inputs
        key_rows = lax.dynamic_slice_in_dim(kv_cache, (prompt * LEN).astype(jnp.int32), LEN, 0).astype(jnp.float32)
        allowed = jnp.arange(LEN, dtype=jnp.int32) < prompt_len[prompt]
        scores = jnp.dot(query_row.astype(jnp.float32), key_rows.T) * score_scale
        scores = jnp.where(allowed[None, :], scores, -1e+30)
        top_score = lax.optimization_barrier(jnp.max(scores, axis=1, keepdims=True))
        weights = jnp.where(allowed[None, :], jnp.exp(scores - top_score), 0.0)
        rounded = lax.optimization_barrier(weights.astype(jnp.bfloat16)).astype(jnp.float32)
        summed = jnp.dot(rounded, key_rows[:, :KV_RANK])
        return (summed / lax.optimization_barrier(jnp.sum(weights, axis=1, keepdims=True))).astype(jnp.bfloat16)
    return lax.map(one_row, (queries, row_prompt))
```

```python
import functools

import jax
import jax.numpy as jnp
from jax import lax
from jax.experimental import pallas as pl
from jax.experimental.pallas import tpu as pltpu
from jax.sharding import PartitionSpec as P

score_scale = 192.0 ** (-0.5)
masked_score = -1e30
VMEM = pltpu.VMEM
whole_vmem = pl.BlockSpec(memory_space=pltpu.VMEM)
whole_smem = pl.BlockSpec(memory_space=pltpu.SMEM)
left_in_place = pl.BlockSpec(memory_space=pl.ANY)


def last_dims_dot(left, right):
    return lax.dot_general(left, right, (((1,), (1,)), ((), ())), preferred_element_type=jnp.float32)


def project_kernel(chunk, first_ref, states_hbm, weights_hbm, partial_ref, angle_ref, states, weights, states_sem, sems):
    depth = states_hbm.shape[1]
    copies = []
    states_copy = pltpu.make_async_copy(states_hbm, states, states_sem)
    states_copy.start()
    for index in range(depth // chunk):
        columns = pl.ds(index * chunk, chunk)
        copy = pltpu.make_async_copy(weights_hbm.at[:, columns], weights.at[:, columns], sems.at[index])
        copy.start()
        copies.append(copy)
    tokens, half = angle_ref.shape[1:]
    position = (first_ref[0] + lax.broadcasted_iota(jnp.int32, (tokens, half), 0)).astype(jnp.float32)
    index = lax.broadcasted_iota(jnp.int32, (tokens, half), 1).astype(jnp.float32)
    inverse = jnp.exp(index * (-2.0 / (2 * half) * 9.210340371976184))
    angles = position * inverse
    angle_ref[0] = jnp.cos(angles)
    angle_ref[1] = jnp.sin(angles)
    states_copy.wait()
    total = None
    for index, copy in enumerate(copies):
        copy.wait()
        columns = pl.ds(index * chunk, chunk)
        part = last_dims_dot(states[:, columns], weights[:, columns])
        total = part if total is None else total + part
    partial_ref[...] = total


def encode_kernel(mine_ref, other_ref, gain_ref, angle_ref, cache_ref):
    rank = gain_ref.shape[1]
    half = angle_ref.shape[2]
    projected = mine_ref[...] + other_ref[...]
    content = projected[:, :rank]
    mean = jnp.mean(content * content, axis=1, keepdims=True)
    cache_ref[:, :rank] = (content * lax.rsqrt(mean + 1e-06) * gain_ref[...]).astype(cache_ref.dtype)
    front = projected[:, rank : rank + half]
    back = projected[:, rank + half :]
    cosine, sine = angle_ref[0], angle_ref[1]
    rotated = jnp.concatenate([front * cosine - back * sine, back * cosine + front * sine], axis=1)
    cache_ref[:, rank:] = rotated.astype(cache_ref.dtype)


def attend_kernel(count, where_ref, query_ref, *refs):
    blocks, out_ref = refs[:count], refs[count]
    rank = out_ref.shape[2]
    limit = where_ref[0]
    for row in range(query_ref.shape[0]):
        query = query_ref[row]
        scores = []
        for index, block in enumerate(blocks):
            score = last_dims_dot(query, block[...]) * score_scale
            position = where_ref[1 + index] + lax.broadcasted_iota(jnp.int32, score.shape, 1)
            scores.append(jnp.where(position < limit, score, masked_score))
        top = functools.reduce(jnp.maximum, [jnp.max(s, axis=1, keepdims=True) for s in scores])
        total, summed = 0.0, 0.0
        for score, block in zip(scores, blocks):
            weights = jnp.exp(score - top)
            total = total + jnp.sum(weights, axis=1, keepdims=True)
            summed = summed + jnp.dot(
                weights.astype(jnp.bfloat16), block[:, :rank], preferred_element_type=jnp.float32
            )
        out_ref[row] = (summed / total).astype(out_ref.dtype)


def per_device(prompt_states, down_kv, kv_gain, queries, row_prompt, prompt_len):
    tokens, depth = prompt_states.shape
    latent = down_kv.shape[1]
    rank = kv_gain.shape[0]
    half = (latent - rank) // 2
    prompts = prompt_len.shape[0]
    pool = lax.axis_size("pool")
    seq_len = tokens * pool // prompts
    block = pool // prompts
    pool_at = lax.axis_index("pool")
    core = lax.axis_index("tp")
    prompt = row_prompt[0]
    shift = prompt ^ (pool_at // block)
    limit = jnp.sum(jnp.where(jnp.arange(prompts, dtype=jnp.int32) == prompt, prompt_len, 0))

    chunk = 512 if depth % 512 == 0 else depth
    first = (pool_at * tokens) % seq_len
    partial, angles = pl.pallas_call(
        functools.partial(project_kernel, chunk),
        out_shape=[
            jax.ShapeDtypeStruct((tokens, latent), jnp.float32),
            jax.ShapeDtypeStruct((2, tokens, half), jnp.float32),
        ],
        in_specs=[whole_smem, left_in_place, left_in_place],
        out_specs=[whole_vmem, whole_vmem],
        scratch_shapes=[
            VMEM((tokens, depth), jnp.bfloat16),
            VMEM((latent, depth), jnp.bfloat16),
            pltpu.SemaphoreType.DMA,
            pltpu.SemaphoreType.DMA((depth // chunk,)),
        ],
        compiler_params=pltpu.CompilerParams(vmem_limit_bytes=16 * 2**20),
        name="project",
    )(first.astype(jnp.int32)[None], prompt_states, down_kv.T)

    other = lax.ppermute(partial, "tp", [(0, 1), (1, 0)])
    cache = pl.pallas_call(
        encode_kernel,
        out_shape=jax.ShapeDtypeStruct((tokens, latent), jnp.bfloat16),
        in_specs=[whole_vmem] * 4,
        out_specs=whole_vmem,
        compiler_params=pltpu.CompilerParams(vmem_limit_bytes=4 * 2**20),
        name="encode",
    )(partial, other, kv_gain[None, :], angles)

    if block == 2 and lax.axis_size("tp") == 2:
        def fetch(step):
            pairs = [
                (pl_at * 2 + c, ((pl_at // 2 ^ step) * 2 + c) * 2 + pl_at % 2)
                for pl_at in range(pool)
                for c in range(2)
            ]
            return lambda rows: lax.ppermute(rows, ("pool", "tp"), pairs)

        here = lax.switch(shift, [fetch(step) for step in range(prompts)], cache)
        there = lax.ppermute(here, "tp", [(0, 1), (1, 0)])
        blocks = [here, there]
        starts = [core * tokens, (1 - core) * tokens]
    else:

        def fetch(step):
            pairs = [(at, at ^ (step * block)) for at in range(pool)]
            return lambda rows: lax.ppermute(rows, "pool", pairs) if step else rows

        here = lax.switch(shift, [fetch(step) for step in range(prompts)], cache)
        groups = [list(range(b * block, (b + 1) * block)) for b in range(prompts)]
        blocks = [lax.all_gather(here, "pool", axis=0, tiled=True, axis_index_groups=groups)]
        starts = [jnp.int32(0)]

    where = jnp.stack([limit, *starts]).astype(jnp.int32)
    return pl.pallas_call(
        functools.partial(attend_kernel, len(blocks)),
        out_shape=jax.ShapeDtypeStruct((queries.shape[0], queries.shape[1], rank), jnp.bfloat16),
        in_specs=[whole_smem] + [whole_vmem] * (1 + len(blocks)),
        out_specs=whole_vmem,
        compiler_params=pltpu.CompilerParams(vmem_limit_bytes=(32 if seq_len > 1024 else 8) * 2**20),
        name="attend",
    )(where, queries, *blocks)


def solution(mesh):
    placed = (
        P(("groups", "pool"), "tp"),
        P("tp", None),
        P(),
        P(("groups", "pool"), "tp", None),
        P(("groups", "pool")),
        P("groups"),
    )
    return jax.shard_map(
        per_device,
        mesh=mesh,
        in_specs=placed,
        out_specs=P(("groups", "pool"), "tp", None),
        check_vma=False,
    )
```

```python
import functools

import jax
import jax.numpy as jnp
from jax import lax
from jax.experimental import pallas as pl
from jax.experimental.pallas import tpu as pltpu
from jax.sharding import PartitionSpec as P

score_scale = 192.0 ** (-0.5)
masked_score = -1e30
VMEM = pltpu.VMEM
whole_vmem = pl.BlockSpec(memory_space=pltpu.VMEM)
whole_smem = pl.BlockSpec(memory_space=pltpu.SMEM)
in_hbm = pl.BlockSpec(memory_space=pltpu.HBM)


def last_dims_dot(left, right):
    return lax.dot_general(left, right, (((1,), (1,)), ((), ())), preferred_element_type=jnp.float32)


def project_kernel(
    chunk, place_ref, owner_hbm, lengths_hbm, states_hbm, weights_hbm, partial_ref, angle_ref, bias_ref, states, weights,
    owner, lengths, states_sem, small_sems, sems
):
    depth = states_hbm.shape[1]
    copies = []
    states_copy = pltpu.make_async_copy(states_hbm, states, states_sem)
    states_copy.start()
    for index in range(depth // chunk):
        columns = pl.ds(index * chunk, chunk)
        copy = pltpu.make_async_copy(weights_hbm.at[:, columns], weights.at[:, columns], sems.at[index])
        copy.start()
        copies.append(copy)
    small = [
        pltpu.make_async_copy(owner_hbm, owner, small_sems.at[0]),
        pltpu.make_async_copy(lengths_hbm, lengths, small_sems.at[1]),
    ]
    for copy in small:
        copy.start()
    tokens, half = angle_ref.shape[1:]
    position = (place_ref[0] + lax.broadcasted_iota(jnp.int32, (tokens, half), 0)).astype(jnp.float32)
    index = lax.broadcasted_iota(jnp.int32, (tokens, half), 1).astype(jnp.float32)
    inverse = jnp.exp(index * (-2.0 / (2 * half) * 9.210340371976184))
    angles = position * inverse
    angle_ref[0] = jnp.cos(angles)
    angle_ref[1] = jnp.sin(angles)
    for copy in small:
        copy.wait()
    seq_len = bias_ref.shape[1]
    limit = lengths[owner[0]]
    slot = place_ref[1] + lax.broadcasted_iota(jnp.int32, bias_ref.shape, 1)
    slot = jnp.where(slot >= seq_len, slot - seq_len, slot)
    bias_ref[...] = jnp.where(slot < limit, 0.0, masked_score)
    states_copy.wait()
    total = None
    for index, copy in enumerate(copies):
        copy.wait()
        columns = pl.ds(index * chunk, chunk)
        part = last_dims_dot(states[:, columns], weights[:, columns])
        total = part if total is None else total + part
    partial_ref[...] = total


def encode_kernel(mine_ref, other_ref, gain_ref, angle_ref, cache_ref):
    rank = gain_ref.shape[1]
    half = angle_ref.shape[2]
    projected = mine_ref[...] + other_ref[...]
    content = projected[:, :rank]
    mean = jnp.mean(content * content, axis=1, keepdims=True)
    cache_ref[:, :rank] = (content * lax.rsqrt(mean + 1e-06) * gain_ref[...]).astype(cache_ref.dtype)
    front = projected[:, rank : rank + half]
    back = projected[:, rank + half :]
    cosine, sine = angle_ref[0], angle_ref[1]
    rotated = jnp.concatenate([front * cosine - back * sine, back * cosine + front * sine], axis=1)
    cache_ref[:, rank:] = rotated.astype(cache_ref.dtype)


def attend_kernel(count, query_ref, bias_ref, *refs):
    blocks, out_hbm, out, keys, sems = refs[:count], *refs[count:]
    rows, heads, rank = out_hbm.shape
    if count > 1:
        step = keys.shape[0] // count
        for index, block in enumerate(blocks):
            keys[pl.ds(index * step, step), :] = block[...]
    else:
        keys = blocks[0]
    together = sems.shape[0]
    per = rows // together
    copies = []
    for part in range(together):
        query = query_ref[part * per : (part + 1) * per].reshape(per * heads, query_ref.shape[2])
        score = last_dims_dot(query, keys[...]) * score_scale + bias_ref[...]
        weights = jnp.exp(score - jnp.max(score, axis=1, keepdims=True))
        total = jnp.sum(weights, axis=1, keepdims=True)
        summed = jnp.dot(
            weights.astype(jnp.bfloat16), keys[:, :rank], preferred_element_type=jnp.float32
        )
        mine = pl.ds(part * per, per)
        out[mine] = (summed / total).astype(out.dtype).reshape(per, heads, rank)
        copy = pltpu.make_async_copy(out.at[mine], out_hbm.at[mine], sems.at[part])
        copy.start()
        copies.append(copy)
    for copy in copies:
        copy.wait()


def per_device(prompt_states, down_kv, kv_gain, queries, row_prompt, prompt_len):
    tokens, depth = prompt_states.shape
    latent = down_kv.shape[1]
    rank = kv_gain.shape[0]
    half = (latent - rank) // 2
    prompts = prompt_len.shape[0]
    pool = lax.axis_size("pool")
    seq_len = tokens * pool // prompts
    block = pool // prompts
    pool_at = lax.axis_index("pool")
    core = lax.axis_index("tp")
    shift = row_prompt[0] ^ (pool_at // block)
    paired = block == 2 and lax.axis_size("tp") == 2

    chunk = 512 if depth % 512 == 0 else depth
    first = (pool_at * tokens) % seq_len
    place = jnp.stack([first, core * tokens if paired else jnp.int32(0)]).astype(jnp.int32)
    partial, angles, bias = pl.pallas_call(
        functools.partial(project_kernel, chunk),
        out_shape=[
            jax.ShapeDtypeStruct((tokens, latent), jnp.float32),
            jax.ShapeDtypeStruct((2, tokens, half), jnp.float32),
            jax.ShapeDtypeStruct((1, seq_len), jnp.float32),
        ],
        in_specs=[whole_smem, in_hbm, in_hbm, in_hbm, in_hbm],
        out_specs=[whole_vmem] * 3,
        scratch_shapes=[
            VMEM((tokens, depth), jnp.bfloat16),
            VMEM((latent, depth), jnp.bfloat16),
            pltpu.SMEM(row_prompt.shape, jnp.int32),
            pltpu.SMEM(prompt_len.shape, jnp.int32),
            pltpu.SemaphoreType.DMA,
            pltpu.SemaphoreType.DMA((2,)),
            pltpu.SemaphoreType.DMA((depth // chunk,)),
        ],
        compiler_params=pltpu.CompilerParams(vmem_limit_bytes=16 * 2**20),
        name="project",
    )(place, *[pltpu.with_memory_space_constraint(x, pltpu.HBM) for x in (row_prompt, prompt_len, prompt_states, down_kv.T)])

    other = lax.ppermute(partial, "tp", [(0, 1), (1, 0)])
    cache = pl.pallas_call(
        encode_kernel,
        out_shape=jax.ShapeDtypeStruct((tokens, latent), jnp.bfloat16),
        in_specs=[whole_vmem] * 4,
        out_specs=whole_vmem,
        compiler_params=pltpu.CompilerParams(vmem_limit_bytes=4 * 2**20),
        name="encode",
    )(partial, other, kv_gain[None, :], angles)

    def attend(*blocks):
        parts = 2 if queries.shape[0] % 2 == 0 else 1
        return pl.pallas_call(
            functools.partial(attend_kernel, len(blocks)),
            out_shape=pltpu.HBM((queries.shape[0], queries.shape[1], rank), jnp.bfloat16),
            in_specs=[whole_vmem] * (2 + len(blocks)),
            out_specs=in_hbm,
            scratch_shapes=[
                VMEM((queries.shape[0], queries.shape[1], rank), jnp.bfloat16),
                VMEM((seq_len if len(blocks) > 1 else 16, latent), jnp.bfloat16),
                pltpu.SemaphoreType.DMA((parts,)),
            ],
            compiler_params=pltpu.CompilerParams(vmem_limit_bytes=(32 if seq_len > 1024 else 8) * 2**20),
            name="attend",
        )(queries, bias, *blocks)

    def paired_step(step):
        pairs = [
            (at * 2 + c, ((at // 2 ^ step) * 2 + c) * 2 + at % 2) for at in range(pool) for c in range(2)
        ]

        def run(rows):
            here = lax.ppermute(rows, ("pool", "tp"), pairs)
            return attend(here, lax.ppermute(here, "tp", [(0, 1), (1, 0)]))

        return run

    if paired:
        return lax.switch(shift, [paired_step(step) for step in range(prompts)], cache)

    def fetch(step):
        pairs = [(at, at ^ (step * block)) for at in range(pool)]
        return lambda rows: lax.ppermute(rows, "pool", pairs) if step else rows

    here = lax.switch(shift, [fetch(step) for step in range(prompts)], cache)
    members = [list(range(b * block, (b + 1) * block)) for b in range(prompts)]
    return attend(lax.all_gather(here, "pool", axis=0, tiled=True, axis_index_groups=members))


def solution(mesh):
    placed = (
        P(("groups", "pool"), "tp"),
        P("tp", None),
        P(),
        P(("groups", "pool"), "tp", None),
        P(("groups", "pool")),
        P("groups"),
    )
    return jax.shard_map(
        per_device,
        mesh=mesh,
        in_specs=placed,
        out_specs=P(("groups", "pool"), "tp", None),
        check_vma=False,
    )
```

```python
import functools

import jax
import jax.numpy as jnp
from jax import lax
from jax.experimental import pallas as pl
from jax.experimental.pallas import tpu as pltpu
from jax.sharding import PartitionSpec as P

score_scale = 192.0 ** (-0.5)
masked_score = -1e30
VMEM = pltpu.VMEM
whole_vmem = pl.BlockSpec(memory_space=pltpu.VMEM)
whole_smem = pl.BlockSpec(memory_space=pltpu.SMEM)
in_hbm = pl.BlockSpec(memory_space=pltpu.HBM)


def last_dims_dot(left, right):
    return lax.dot_general(left, right, (((1,), (1,)), ((), ())), preferred_element_type=jnp.float32)


def project_kernel(chunk, states_hbm, weights_hbm, partial_ref, states, weights, states_sem, sems):
    depth = states_hbm.shape[1]
    states_copy = pltpu.make_async_copy(states_hbm, states, states_sem)
    states_copy.start()
    copies = []
    for index in range(depth // chunk):
        columns = pl.ds(index * chunk, chunk)
        copy = pltpu.make_async_copy(weights_hbm.at[:, columns], weights.at[:, columns], sems.at[index])
        copy.start(priority=1)
        copies.append(copy)
    states_copy.wait()
    total = None
    for index, copy in enumerate(copies):
        copy.wait()
        columns = pl.ds(index * chunk, chunk)
        part = last_dims_dot(states[:, columns], weights[:, columns])
        total = part if total is None else total + part
    partial_ref[...] = total


def angle_kernel(seq_len, cosine_ref, sine_ref):
    tokens, width = cosine_ref.shape
    half = width // 2
    first = lax.rem(lax.axis_index("pool") * tokens, seq_len)
    position = (first + lax.broadcasted_iota(jnp.int32, (tokens, width), 0)).astype(jnp.float32)
    column = lax.broadcasted_iota(jnp.int32, (tokens, width), 1)
    front = column < half
    index = jnp.where(front, column, column - half).astype(jnp.float32)
    angles = position * jnp.exp(index * (-2.0 / width * 9.210340371976184))
    cosine_ref[...] = jnp.cos(angles)
    sine = jnp.sin(angles)
    sine_ref[...] = jnp.where(front, -sine, sine)


def mask_kernel(swap, owner_hbm, lengths_hbm, bias_ref, owner, lengths, sems):
    small = [
        pltpu.make_async_copy(owner_hbm, owner, sems.at[0]),
        pltpu.make_async_copy(lengths_hbm, lengths, sems.at[1]),
    ]
    for copy in small:
        copy.start()
    seq_len = bias_ref.shape[1]
    slot = lax.broadcasted_iota(jnp.int32, bias_ref.shape, 1)
    if swap:
        start = lax.rem(lax.axis_index("pool") + lax.axis_index("tp"), 2) * (seq_len // 2)
        slot = slot + start
        slot = jnp.where(slot >= seq_len, slot - seq_len, slot)
    for copy in small:
        copy.wait()
    bias_ref[...] = jnp.where(slot < lengths[owner[0]], 0.0, masked_score)


def encode_kernel(mine_ref, other_ref, gain_ref, cosine_ref, sine_ref, cache_ref):
    rank = gain_ref.shape[1]
    half = cosine_ref.shape[1] // 2
    projected = mine_ref[...] + other_ref[...]
    content = projected[:, :rank]
    mean = jnp.mean(content * content, axis=1, keepdims=True)
    cache_ref[:, :rank] = (content * lax.rsqrt(mean + 1e-06) * gain_ref[...]).astype(cache_ref.dtype)
    rotary = projected[:, rank:]
    swapped = jnp.concatenate([rotary[:, half:], rotary[:, :half]], axis=1)
    cache_ref[:, rank:] = (rotary * cosine_ref[...] + swapped * sine_ref[...]).astype(cache_ref.dtype)


def attend_kernel(count, query_ref, bias_ref, *refs):
    blocks, out_hbm, out, keys, sems = refs[:count], *refs[count:]
    rows, heads, rank = out_hbm.shape
    if count > 1:
        step = keys.shape[0] // count
        for index, block in enumerate(blocks):
            keys[pl.ds(index * step, step), :] = block[...]
    else:
        keys = blocks[0]
    query = query_ref[...].reshape(rows * heads, query_ref.shape[2])
    score = last_dims_dot(query, keys[...]) * score_scale + bias_ref[...]
    weights = jnp.exp(score - jnp.max(score, axis=1, keepdims=True))
    inverse = 1.0 / jnp.sum(weights, axis=1, keepdims=True)
    rounded = weights.astype(jnp.bfloat16)
    parts = sems.shape[0]
    per = rows // parts
    copies = []
    for part in range(parts):
        lines = slice(part * per * heads, (part + 1) * per * heads)
        summed = jnp.dot(rounded[lines], keys[:, :rank], preferred_element_type=jnp.float32)
        mine = pl.ds(part * per, per)
        out[mine] = (summed * inverse[lines]).astype(out.dtype).reshape(per, heads, rank)
        copy = pltpu.make_async_copy(out.at[mine], out_hbm.at[mine], sems.at[part])
        copy.start()
        copies.append(copy)
    for copy in copies:
        copy.wait()


def per_device(prompt_states, down_kv, kv_gain, queries, row_prompt, prompt_len):
    tokens, depth = prompt_states.shape
    latent = down_kv.shape[1]
    rank = kv_gain.shape[0]
    half = (latent - rank) // 2
    prompts = prompt_len.shape[0]
    pool = lax.axis_size("pool")
    seq_len = tokens * pool // prompts
    block = pool // prompts
    pool_at = lax.axis_index("pool")
    core = lax.axis_index("tp")
    shift = row_prompt[0] ^ (pool_at // block)
    paired = block == 2 and lax.axis_size("tp") == 2

    chunk = 512 if depth % 512 == 0 else depth
    hbm = functools.partial(pltpu.with_memory_space_constraint, memory_space=pltpu.HBM)
    partial = pl.pallas_call(
        functools.partial(project_kernel, chunk),
        out_shape=jax.ShapeDtypeStruct((tokens, latent), jnp.float32),
        in_specs=[in_hbm, in_hbm],
        out_specs=whole_vmem,
        scratch_shapes=[
            VMEM((tokens, depth), jnp.bfloat16),
            VMEM((latent, depth), jnp.bfloat16),
            pltpu.SemaphoreType.DMA,
            pltpu.SemaphoreType.DMA((depth // chunk,)),
        ],
        compiler_params=pltpu.CompilerParams(vmem_limit_bytes=16 * 2**20),
        cost_estimate=pl.CostEstimate(flops=2 * tokens * depth * latent, bytes_accessed=2 * depth * (latent + tokens), transcendentals=0),
        name="project",
    )(hbm(prompt_states), hbm(down_kv.T))
    cosine, sine = pl.pallas_call(
        functools.partial(angle_kernel, seq_len),
        out_shape=[jax.ShapeDtypeStruct((tokens, 2 * half), jnp.float32)] * 2,
        out_specs=[whole_vmem] * 2,
        compiler_params=pltpu.CompilerParams(vmem_limit_bytes=4 * 2**20),
        cost_estimate=pl.CostEstimate(flops=100 * tokens * half, bytes_accessed=4096, transcendentals=4 * tokens * half),
        name="angles",
    )()

    other = lax.ppermute(partial, "tp", [(0, 1), (1, 0)])
    cache = pl.pallas_call(
        encode_kernel,
        out_shape=jax.ShapeDtypeStruct((tokens, latent), jnp.bfloat16),
        in_specs=[whole_vmem] * 5,
        out_specs=whole_vmem,
        compiler_params=pltpu.CompilerParams(vmem_limit_bytes=4 * 2**20),
        name="encode",
    )(partial, other, kv_gain[None, :], cosine, sine)

    def mask():
        return pl.pallas_call(
            functools.partial(mask_kernel, paired),
            out_shape=jax.ShapeDtypeStruct((1, seq_len), jnp.float32),
            in_specs=[in_hbm, in_hbm],
            out_specs=whole_vmem,
            scratch_shapes=[
                pltpu.SMEM(row_prompt.shape, jnp.int32),
                pltpu.SMEM(prompt_len.shape, jnp.int32),
                pltpu.SemaphoreType.DMA((2,)),
            ],
            compiler_params=pltpu.CompilerParams(vmem_limit_bytes=4 * 2**20),
            cost_estimate=pl.CostEstimate(flops=1000, bytes_accessed=4096, transcendentals=0),
            name="mask",
        )(hbm(row_prompt), hbm(prompt_len))

    def attend(bias, *blocks):
        parts = 2 if queries.shape[0] % 2 == 0 else 1
        return pl.pallas_call(
            functools.partial(attend_kernel, len(blocks)),
            out_shape=pltpu.HBM((queries.shape[0], queries.shape[1], rank), jnp.bfloat16),
            in_specs=[whole_vmem] * (2 + len(blocks)),
            out_specs=in_hbm,
            scratch_shapes=[
                VMEM((queries.shape[0], queries.shape[1], rank), jnp.bfloat16),
                VMEM((seq_len if len(blocks) > 1 else 16, latent), jnp.bfloat16),
                pltpu.SemaphoreType.DMA((parts,)),
            ],
            compiler_params=pltpu.CompilerParams(vmem_limit_bytes=(32 if seq_len > 1024 else 8) * 2**20),
            name="attend",
        )(queries, bias, *blocks)

    def paired_step(step):
        pairs = [
            (at * 2 + c, ((at // 2 ^ step) * 2 + (at % 2 ^ c)) * 2 + c) for at in range(pool) for c in range(2)
        ]

        def run(rows):
            if step == 0:
                there = lax.ppermute(rows, "pool", [(at, at ^ 1) for at in range(pool)])
                return attend(mask(), jnp.where(core == 0, rows, there), jnp.where(core == 0, there, rows))
            here = lax.ppermute(rows, ("pool", "tp"), pairs)
            return attend(mask(), here, lax.ppermute(here, "tp", [(0, 1), (1, 0)]))

        return run

    if paired:
        return lax.switch(shift, [paired_step(step) for step in range(prompts)], cache)

    def fetch(step):
        pairs = [(at, at ^ (step * block)) for at in range(pool)]
        return lambda rows: lax.ppermute(rows, "pool", pairs) if step else rows

    here = lax.switch(shift, [fetch(step) for step in range(prompts)], cache)
    members = [list(range(b * block, (b + 1) * block)) for b in range(prompts)]
    return attend(mask(), lax.all_gather(here, "pool", axis=0, tiled=True, axis_index_groups=members))


def solution(mesh):
    placed = (
        P(("groups", "pool"), "tp"),
        P("tp", None),
        P(),
        P(("groups", "pool"), "tp", None),
        P(("groups", "pool")),
        P("groups"),
    )
    return jax.shard_map(
        per_device,
        mesh=mesh,
        in_specs=placed,
        out_specs=P(("groups", "pool"), "tp", None),
        check_vma=False,
    )
```

```python
import functools

import jax
import jax.numpy as jnp
from jax import lax
from jax.experimental import pallas as pl
from jax.experimental.pallas import tpu as pltpu
from jax.sharding import PartitionSpec as P

score_scale = 192.0 ** (-0.5)
masked_score = -1e30
lanes = 128
VMEM = pltpu.VMEM
whole_vmem = pl.BlockSpec(memory_space=pltpu.VMEM)
whole_smem = pl.BlockSpec(memory_space=pltpu.SMEM)
in_hbm = pl.BlockSpec(memory_space=pltpu.HBM)


def last_dims_dot(left, right):
    return lax.dot_general(left, right, (((1,), (1,)), ((), ())), preferred_element_type=jnp.float32)


def project_kernel(chunk, states_hbm, weights_hbm, partial_ref, states, weights, states_sem, sems):
    depth = states_hbm.shape[1]
    states_copy = pltpu.make_async_copy(states_hbm, states, states_sem)
    states_copy.start()
    copies = []
    for index in range(depth // chunk):
        columns = pl.ds(index * chunk, chunk)
        copy = pltpu.make_async_copy(weights_hbm.at[:, columns], weights.at[:, columns], sems.at[index])
        copy.start(priority=1)
        copies.append(copy)
    states_copy.wait()
    total = None
    for index, copy in enumerate(copies):
        copy.wait()
        columns = pl.ds(index * chunk, chunk)
        part = last_dims_dot(states[:, columns], weights[:, columns])
        total = part if total is None else total + part
    partial_ref[...] = total


def angle_kernel(seq_len, cosine_ref, sine_ref):
    tokens, width = cosine_ref.shape
    half = width // 2
    first = lax.rem(lax.axis_index("pool") * tokens, seq_len)
    position = (first + lax.broadcasted_iota(jnp.int32, (tokens, width), 0)).astype(jnp.float32)
    column = lax.broadcasted_iota(jnp.int32, (tokens, width), 1)
    front = column < half
    index = jnp.where(front, column, column - half).astype(jnp.float32)
    angles = position * jnp.exp(index * (-2.0 / width * 9.210340371976184))
    cosine_ref[...] = jnp.cos(angles)
    sine = jnp.sin(angles)
    sine_ref[...] = jnp.where(front, -sine, sine)


def mask_kernel(axes, owner_hbm, lengths_hbm, bias_ref, owner, lengths, sems):
    small = [
        pltpu.make_async_copy(owner_hbm, owner, sems.at[0]),
        pltpu.make_async_copy(lengths_hbm, lengths, sems.at[1]),
    ]
    for copy in small:
        copy.start()
    seq_len = bias_ref.shape[1]
    slot = lax.broadcasted_iota(jnp.int32, bias_ref.shape, 1)
    if axes:
        slot = slot + lax.rem(sum(lax.axis_index(axis) for axis in axes), 2) * (seq_len // 2)
        slot = jnp.where(slot >= seq_len, slot - seq_len, slot)
    for copy in small:
        copy.wait()
    bias_ref[...] = jnp.where(slot < lengths[owner[0]], 0.0, masked_score)


def encode_kernel(packed, mine_ref, other_ref, gain_ref, cosine_ref, sine_ref, cache_ref):
    rank = gain_ref.shape[1]
    tokens, width = cosine_ref.shape
    projected = mine_ref[...] + other_ref[...]
    content = projected[:, :rank]
    mean = jnp.mean(content * content, axis=1, keepdims=True)
    normed = (content * lax.rsqrt(mean + 1e-06) * gain_ref[...]).astype(cache_ref.dtype)
    rotary = projected[:, rank:]
    swapped = jnp.concatenate([rotary[:, width // 2 :], rotary[:, : width // 2]], axis=1)
    rotated = rotary * cosine_ref[...] + swapped * sine_ref[...]
    if packed:
        for index in range(rank // lanes):
            cache_ref[index * tokens : (index + 1) * tokens, :] = normed[:, index * lanes : (index + 1) * lanes]
        paired_rows = jnp.concatenate([rotated[: tokens // 2], rotated[tokens // 2 :]], axis=1)
        cache_ref[rank // lanes * tokens :, :] = paired_rows.astype(cache_ref.dtype)
    else:
        cache_ref[:, :rank] = normed
        cache_ref[:, rank:] = rotated.astype(cache_ref.dtype)


def attend_kernel(packed, query_ref, bias_ref, *refs):
    count = 2 if packed else 1
    blocks, out_hbm, out, keys, sems = refs[:count], *refs[count:]
    rows, heads, rank = out_hbm.shape
    if packed:
        tokens = keys.shape[0] // 2
        width = keys.shape[1] - rank
        for half, block in enumerate(blocks):
            first = half * tokens
            for index in range(rank // lanes):
                keys[first : first + tokens, index * lanes : (index + 1) * lanes] = block[
                    index * tokens : (index + 1) * tokens, :
                ]
            paired_rows = block[rank // lanes * tokens :, :]
            keys[first : first + tokens // 2, rank:] = paired_rows[:, :width]
            keys[first + tokens // 2 : first + tokens, rank:] = paired_rows[:, width:]
    else:
        keys = blocks[0]
    query = query_ref[...].reshape(rows * heads, query_ref.shape[2])
    score = last_dims_dot(query, keys[...]) * score_scale + bias_ref[...]
    weights = jnp.exp(score - jnp.max(score, axis=1, keepdims=True))
    inverse = 1.0 / jnp.sum(weights, axis=1, keepdims=True)
    rounded = weights.astype(jnp.bfloat16)
    parts = sems.shape[0]
    per = rows // parts
    copies = []
    for part in range(parts):
        lines = slice(part * per * heads, (part + 1) * per * heads)
        summed = jnp.dot(rounded[lines], keys[:, :rank], preferred_element_type=jnp.float32)
        mine = pl.ds(part * per, per)
        out[mine] = (summed * inverse[lines]).astype(out.dtype).reshape(per, heads, rank)
        copy = pltpu.make_async_copy(out.at[mine], out_hbm.at[mine], sems.at[part])
        copy.start()
        copies.append(copy)
    for copy in copies:
        copy.wait()


def per_device(prompt_states, down_kv, kv_gain, queries, row_prompt, prompt_len):
    tokens, depth = prompt_states.shape
    latent = down_kv.shape[1]
    rank = kv_gain.shape[0]
    half = (latent - rank) // 2
    prompts = prompt_len.shape[0]
    pool = lax.axis_size("pool")
    seq_len = tokens * pool // prompts
    block = pool // prompts
    pool_at = lax.axis_index("pool")
    shift = row_prompt[0] ^ (pool_at // block)
    packed = block == 2 and lax.axis_size("tp") == 2 and rank % lanes == 0 and 4 * half == lanes and tokens % 32 == 0
    cache_shape = (tokens * latent // lanes, lanes) if packed else (tokens, latent)

    chunk = 512 if depth % 512 == 0 else depth
    hbm = functools.partial(pltpu.with_memory_space_constraint, memory_space=pltpu.HBM)
    partial = pl.pallas_call(
        functools.partial(project_kernel, chunk),
        out_shape=jax.ShapeDtypeStruct((tokens, latent), jnp.float32),
        in_specs=[in_hbm, in_hbm],
        out_specs=whole_vmem,
        scratch_shapes=[
            VMEM((tokens, depth), jnp.bfloat16),
            VMEM((latent, depth), jnp.bfloat16),
            pltpu.SemaphoreType.DMA,
            pltpu.SemaphoreType.DMA((depth // chunk,)),
        ],
        compiler_params=pltpu.CompilerParams(vmem_limit_bytes=16 * 2**20),
        cost_estimate=pl.CostEstimate(flops=2 * tokens * depth * latent, bytes_accessed=2 * depth * (latent + tokens), transcendentals=0),
        name="project",
    )(hbm(prompt_states), hbm(down_kv.T))
    cosine, sine = pl.pallas_call(
        functools.partial(angle_kernel, seq_len),
        out_shape=[jax.ShapeDtypeStruct((tokens, 2 * half), jnp.float32)] * 2,
        out_specs=[whole_vmem] * 2,
        compiler_params=pltpu.CompilerParams(vmem_limit_bytes=4 * 2**20),
        cost_estimate=pl.CostEstimate(flops=100 * tokens * half, bytes_accessed=4096, transcendentals=4 * tokens * half),
        name="angles",
    )()

    other = lax.ppermute(partial, "tp", [(0, 1), (1, 0)])
    cache = pl.pallas_call(
        functools.partial(encode_kernel, packed),
        out_shape=jax.ShapeDtypeStruct(cache_shape, jnp.bfloat16),
        in_specs=[whole_vmem] * 5,
        out_specs=whole_vmem,
        compiler_params=pltpu.CompilerParams(vmem_limit_bytes=4 * 2**20),
        name="encode",
    )(partial, other, kv_gain[None, :], cosine, sine)

    def mask(*axes):
        return pl.pallas_call(
            functools.partial(mask_kernel, axes),
            out_shape=jax.ShapeDtypeStruct((1, seq_len), jnp.float32),
            in_specs=[in_hbm, in_hbm],
            out_specs=whole_vmem,
            scratch_shapes=[
                pltpu.SMEM(row_prompt.shape, jnp.int32),
                pltpu.SMEM(prompt_len.shape, jnp.int32),
                pltpu.SemaphoreType.DMA((2,)),
            ],
            compiler_params=pltpu.CompilerParams(vmem_limit_bytes=4 * 2**20),
            cost_estimate=pl.CostEstimate(flops=1000, bytes_accessed=4096, transcendentals=0),
            name="mask",
        )(hbm(row_prompt), hbm(prompt_len))

    def attend(bias, *blocks):
        parts = 2 if queries.shape[0] % 2 == 0 else 1
        return pl.pallas_call(
            functools.partial(attend_kernel, len(blocks) > 1),
            out_shape=pltpu.HBM((queries.shape[0], queries.shape[1], rank), jnp.bfloat16),
            in_specs=[whole_vmem] * (2 + len(blocks)),
            out_specs=in_hbm,
            scratch_shapes=[
                VMEM((queries.shape[0], queries.shape[1], rank), jnp.bfloat16),
                VMEM((seq_len if len(blocks) > 1 else 16, latent), jnp.bfloat16),
                pltpu.SemaphoreType.DMA((parts,)),
            ],
            compiler_params=pltpu.CompilerParams(vmem_limit_bytes=(32 if seq_len > 1024 else 8) * 2**20),
            name="attend",
        )(queries, bias, *blocks)

    def paired_step(step):
        pairs = [
            (at * 2 + c, ((at // 2 ^ step) * 2 + (at % 2 ^ c)) * 2 + c) for at in range(pool) for c in range(2)
        ]

        def run(rows):
            if step == 0:
                there = lax.ppermute(rows, "pool", [(at, at ^ 1) for at in range(pool)])
                return attend(mask("pool"), rows, there)
            here = lax.ppermute(rows, ("pool", "tp"), pairs)
            return attend(mask("pool", "tp"), here, lax.ppermute(here, "tp", [(0, 1), (1, 0)]))

        return run

    if packed:
        return lax.switch(shift, [paired_step(step) for step in range(prompts)], cache)

    def fetch(step):
        pairs = [(at, at ^ (step * block)) for at in range(pool)]
        return lambda rows: lax.ppermute(rows, "pool", pairs) if step else rows

    here = lax.switch(shift, [fetch(step) for step in range(prompts)], cache)
    members = [list(range(b * block, (b + 1) * block)) for b in range(prompts)]
    return attend(mask(), lax.all_gather(here, "pool", axis=0, tiled=True, axis_index_groups=members))


def solution(mesh):
    placed = (
        P(("groups", "pool"), "tp"),
        P("tp", None),
        P(),
        P(("groups", "pool"), "tp", None),
        P(("groups", "pool")),
        P("groups"),
    )
    return jax.shard_map(
        per_device,
        mesh=mesh,
        in_specs=placed,
        out_specs=P(("groups", "pool"), "tp", None),
        check_vma=False,
    )
```

```python
import functools

import jax
import jax.numpy as jnp
from jax import lax
from jax.experimental import pallas as pl
from jax.experimental.pallas import tpu as pltpu
from jax.sharding import PartitionSpec as P

score_scale = 192.0 ** (-0.5)
masked_score = -1e30
lanes = 128
VMEM = pltpu.VMEM
whole_vmem = pl.BlockSpec(memory_space=pltpu.VMEM)
whole_smem = pl.BlockSpec(memory_space=pltpu.SMEM)
in_hbm = pl.BlockSpec(memory_space=pltpu.HBM)


def last_dims_dot(left, right):
    return lax.dot_general(left, right, (((1,), (1,)), ((), ())), preferred_element_type=jnp.float32)


def project_kernel(chunk, states_hbm, weights_hbm, partial_ref, states, weights, states_sem, sems):
    depth = states_hbm.shape[1]
    states_copy = pltpu.make_async_copy(states_hbm, states, states_sem)
    states_copy.start()
    copies = []
    for index in range(depth // chunk):
        columns = pl.ds(index * chunk, chunk)
        copy = pltpu.make_async_copy(weights_hbm.at[:, columns], weights.at[:, columns], sems.at[index])
        copy.start(priority=1)
        copies.append(copy)
    states_copy.wait()
    total = None
    for index, copy in enumerate(copies):
        copy.wait()
        columns = pl.ds(index * chunk, chunk)
        part = last_dims_dot(states[:, columns], weights[:, columns])
        total = part if total is None else total + part
    partial_ref[...] = total


def angle_kernel(seq_len, cosine_ref, sine_ref):
    tokens, width = cosine_ref.shape
    half = width // 2
    first = lax.rem(lax.axis_index("pool") * tokens, seq_len)
    position = (first + lax.broadcasted_iota(jnp.int32, (tokens, width), 0)).astype(jnp.float32)
    column = lax.broadcasted_iota(jnp.int32, (tokens, width), 1)
    front = column < half
    index = jnp.where(front, column, column - half).astype(jnp.float32)
    angles = position * jnp.exp(index * (-2.0 / width * 9.210340371976184))
    cosine_ref[...] = jnp.cos(angles)
    sine = jnp.sin(angles)
    sine_ref[...] = jnp.where(front, -sine, sine)


def mask_kernel(axes, owner_hbm, lengths_hbm, query_hbm, bias_ref, query_ref, owner, lengths, sems):
    small = [
        pltpu.make_async_copy(owner_hbm, owner, sems.at[0]),
        pltpu.make_async_copy(lengths_hbm, lengths, sems.at[1]),
    ]
    fetch = pltpu.make_async_copy(query_hbm, query_ref, sems.at[2])
    for copy in [*small, fetch]:
        copy.start()
    seq_len = bias_ref.shape[1]
    slot = lax.broadcasted_iota(jnp.int32, bias_ref.shape, 1)
    if axes:
        slot = slot + lax.rem(sum(lax.axis_index(axis) for axis in axes), 2) * (seq_len // 2)
        slot = jnp.where(slot >= seq_len, slot - seq_len, slot)
    for copy in small:
        copy.wait()
    bias_ref[...] = jnp.where(slot < lengths[owner[0]], 0.0, masked_score)
    fetch.wait()


def encode_kernel(packed, mine_ref, other_ref, gain_ref, cosine_ref, sine_ref, cache_ref):
    rank = gain_ref.shape[1]
    tokens, width = cosine_ref.shape
    projected = mine_ref[...] + other_ref[...]
    content = projected[:, :rank]
    mean = jnp.mean(content * content, axis=1, keepdims=True)
    normed = (content * lax.rsqrt(mean + 1e-06) * gain_ref[...]).astype(cache_ref.dtype)
    rotary = projected[:, rank:]
    swapped = jnp.concatenate([rotary[:, width // 2 :], rotary[:, : width // 2]], axis=1)
    rotated = rotary * cosine_ref[...] + swapped * sine_ref[...]
    if packed:
        for index in range(rank // lanes):
            cache_ref[index * tokens : (index + 1) * tokens, :] = normed[:, index * lanes : (index + 1) * lanes]
        paired_rows = jnp.concatenate([rotated[: tokens // 2], rotated[tokens // 2 :]], axis=1)
        cache_ref[rank // lanes * tokens :, :] = paired_rows.astype(cache_ref.dtype)
    else:
        cache_ref[:, :rank] = normed
        cache_ref[:, rank:] = rotated.astype(cache_ref.dtype)


def attend_kernel(packed, query_ref, bias_ref, *refs):
    count = 2 if packed else 1
    blocks, out_hbm, out, keys, sems = refs[:count], *refs[count:]
    rows, heads, rank = out_hbm.shape
    if packed:
        tokens = keys.shape[0] // 2
        width = keys.shape[1] - rank
        for half, block in enumerate(blocks):
            first = half * tokens
            for index in range(rank // lanes):
                keys[first : first + tokens, index * lanes : (index + 1) * lanes] = block[
                    index * tokens : (index + 1) * tokens, :
                ]
            paired_rows = block[rank // lanes * tokens :, :]
            keys[first : first + tokens // 2, rank:] = paired_rows[:, :width]
            keys[first + tokens // 2 : first + tokens, rank:] = paired_rows[:, width:]
    else:
        keys = blocks[0]
    query = query_ref[...].reshape(rows * heads, query_ref.shape[2])
    parts = sems.shape[0]
    per = rows // parts
    spans = [slice(part * per * heads, (part + 1) * per * heads) for part in range(parts)]
    products = [last_dims_dot(query[span], keys[...]) for span in spans]
    rounded, inverse = [], []
    for product in products:
        score = product * score_scale + bias_ref[...]
        weights = jnp.exp(score - jnp.max(score, axis=1, keepdims=True))
        inverse.append(1.0 / jnp.sum(weights, axis=1, keepdims=True))
        rounded.append(weights.astype(jnp.bfloat16))
    sums = [jnp.dot(part, keys[:, :rank], preferred_element_type=jnp.float32) for part in rounded]
    copies = []
    for part in range(parts):
        mine = pl.ds(part * per, per)
        out[mine] = (sums[part] * inverse[part]).astype(out.dtype).reshape(per, heads, rank)
        copy = pltpu.make_async_copy(out.at[mine], out_hbm.at[mine], sems.at[part])
        copy.start()
        copies.append(copy)
    for copy in copies:
        copy.wait()


def per_device(prompt_states, down_kv, kv_gain, queries, row_prompt, prompt_len):
    tokens, depth = prompt_states.shape
    latent = down_kv.shape[1]
    rank = kv_gain.shape[0]
    half = (latent - rank) // 2
    prompts = prompt_len.shape[0]
    pool = lax.axis_size("pool")
    seq_len = tokens * pool // prompts
    block = pool // prompts
    pool_at = lax.axis_index("pool")
    shift = row_prompt[0] ^ (pool_at // block)
    packed = block == 2 and lax.axis_size("tp") == 2 and rank % lanes == 0 and 4 * half == lanes and tokens % 32 == 0
    cache_shape = (tokens * latent // lanes, lanes) if packed else (tokens, latent)

    chunk = 512 if depth % 512 == 0 else depth
    hbm = functools.partial(pltpu.with_memory_space_constraint, memory_space=pltpu.HBM)
    partial = pl.pallas_call(
        functools.partial(project_kernel, chunk),
        out_shape=jax.ShapeDtypeStruct((tokens, latent), jnp.float32),
        in_specs=[in_hbm, in_hbm],
        out_specs=whole_vmem,
        scratch_shapes=[
            VMEM((tokens, depth), jnp.bfloat16),
            VMEM((latent, depth), jnp.bfloat16),
            pltpu.SemaphoreType.DMA,
            pltpu.SemaphoreType.DMA((depth // chunk,)),
        ],
        compiler_params=pltpu.CompilerParams(vmem_limit_bytes=16 * 2**20),
        cost_estimate=pl.CostEstimate(flops=2 * tokens * depth * latent, bytes_accessed=2 * depth * (latent + tokens), transcendentals=0),
        name="project",
    )(hbm(prompt_states), hbm(down_kv.T))
    cosine, sine = pl.pallas_call(
        functools.partial(angle_kernel, seq_len),
        out_shape=[jax.ShapeDtypeStruct((tokens, 2 * half), jnp.float32)] * 2,
        out_specs=[whole_vmem] * 2,
        compiler_params=pltpu.CompilerParams(vmem_limit_bytes=4 * 2**20),
        cost_estimate=pl.CostEstimate(flops=100 * tokens * half, bytes_accessed=4096, transcendentals=4 * tokens * half),
        name="angles",
    )()

    other = lax.ppermute(partial, "tp", [(0, 1), (1, 0)])
    cache = pl.pallas_call(
        functools.partial(encode_kernel, packed),
        out_shape=jax.ShapeDtypeStruct(cache_shape, jnp.bfloat16),
        in_specs=[whole_vmem] * 5,
        out_specs=whole_vmem,
        compiler_params=pltpu.CompilerParams(vmem_limit_bytes=4 * 2**20),
        name="encode",
    )(partial, other, kv_gain[None, :], cosine, sine)

    def mask(*axes):
        return pl.pallas_call(
            functools.partial(mask_kernel, axes),
            out_shape=[
                jax.ShapeDtypeStruct((1, seq_len), jnp.float32),
                pltpu.VMEM(queries.shape, queries.dtype),
            ],
            in_specs=[in_hbm] * 3,
            out_specs=[whole_vmem] * 2,
            scratch_shapes=[
                pltpu.SMEM(row_prompt.shape, jnp.int32),
                pltpu.SMEM(prompt_len.shape, jnp.int32),
                pltpu.SemaphoreType.DMA((3,)),
            ],
            compiler_params=pltpu.CompilerParams(vmem_limit_bytes=4 * 2**20),
            cost_estimate=pl.CostEstimate(flops=1000, bytes_accessed=4096, transcendentals=0),
            name="mask_and_queries",
        )(hbm(row_prompt), hbm(prompt_len), hbm(queries))

    def attend(ready, *blocks):
        bias, fetched = ready
        parts = 2 if queries.shape[0] % 2 == 0 else 1
        return pl.pallas_call(
            functools.partial(attend_kernel, len(blocks) > 1),
            out_shape=pltpu.HBM((queries.shape[0], queries.shape[1], rank), jnp.bfloat16),
            in_specs=[whole_vmem] * (2 + len(blocks)),
            out_specs=in_hbm,
            scratch_shapes=[
                VMEM((queries.shape[0], queries.shape[1], rank), jnp.bfloat16),
                VMEM((seq_len if len(blocks) > 1 else 16, latent), jnp.bfloat16),
                pltpu.SemaphoreType.DMA((parts,)),
            ],
            compiler_params=pltpu.CompilerParams(vmem_limit_bytes=(32 if seq_len > 1024 else 8) * 2**20),
            name="attend",
        )(fetched, bias, *blocks)

    def paired_step(step):
        pairs = [
            (at * 2 + c, ((at // 2 ^ step) * 2 + (at % 2 ^ c)) * 2 + c) for at in range(pool) for c in range(2)
        ]

        def run(rows):
            if step == 0:
                there = lax.ppermute(rows, "pool", [(at, at ^ 1) for at in range(pool)])
                return attend(mask("pool"), rows, there)
            here = lax.ppermute(rows, ("pool", "tp"), pairs)
            here, bias = lax.optimization_barrier((here, mask("pool", "tp")))
            return attend(bias, here, lax.ppermute(here, "tp", [(0, 1), (1, 0)]))

        return run

    if packed:
        return lax.switch(shift, [paired_step(step) for step in range(prompts)], cache)

    def fetch(step):
        pairs = [(at, at ^ (step * block)) for at in range(pool)]
        return lambda rows: lax.ppermute(rows, "pool", pairs) if step else rows

    here = lax.switch(shift, [fetch(step) for step in range(prompts)], cache)
    members = [list(range(b * block, (b + 1) * block)) for b in range(prompts)]
    return attend(mask(), lax.all_gather(here, "pool", axis=0, tiled=True, axis_index_groups=members))


def solution(mesh):
    placed = (
        P(("groups", "pool"), "tp"),
        P("tp", None),
        P(),
        P(("groups", "pool"), "tp", None),
        P(("groups", "pool")),
        P("groups"),
    )
    return jax.shard_map(
        per_device,
        mesh=mesh,
        in_specs=placed,
        out_specs=P(("groups", "pool"), "tp", None),
        check_vma=False,
    )
```

```python
import functools

import jax
import jax.numpy as jnp
from jax import lax
from jax.experimental import pallas as pl
from jax.experimental.pallas import tpu as pltpu
from jax.sharding import PartitionSpec as P

score_scale = 192.0 ** (-0.5)
masked_score = -1e30
lanes = 128
VMEM = pltpu.VMEM
whole_vmem = pl.BlockSpec(memory_space=pltpu.VMEM)
whole_smem = pl.BlockSpec(memory_space=pltpu.SMEM)
in_hbm = pl.BlockSpec(memory_space=pltpu.HBM)


def last_dims_dot(left, right):
    return lax.dot_general(left, right, (((1,), (1,)), ((), ())), preferred_element_type=jnp.float32)


def project_kernel(spans, states_hbm, weights_hbm, partial_ref, states, weights, states_sem, sems):
    states_copy = pltpu.make_async_copy(states_hbm, states, states_sem)
    states_copy.start()
    copies = []
    for index, (first, width) in enumerate(spans):
        columns = pl.ds(first, width)
        copy = pltpu.make_async_copy(weights_hbm.at[:, columns], weights.at[:, columns], sems.at[index])
        copy.start(priority=1)
        copies.append(copy)
    states_copy.wait()
    total = None
    for (first, width), copy in zip(spans, copies):
        copy.wait()
        columns = pl.ds(first, width)
        part = last_dims_dot(states[:, columns], weights[:, columns])
        total = part if total is None else total + part
    partial_ref[...] = total


def angle_kernel(seq_len, cosine_ref, sine_ref):
    tokens, width = cosine_ref.shape
    half = width // 2
    first = lax.rem(lax.axis_index("pool") * tokens, seq_len)
    position = (first + lax.broadcasted_iota(jnp.int32, (tokens, width), 0)).astype(jnp.float32)
    column = lax.broadcasted_iota(jnp.int32, (tokens, width), 1)
    front = column < half
    index = jnp.where(front, column, column - half).astype(jnp.float32)
    angles = position * jnp.exp(index * (-2.0 / width * 9.210340371976184))
    cosine_ref[...] = jnp.cos(angles)
    sine = jnp.sin(angles)
    sine_ref[...] = jnp.where(front, -sine, sine)


def mask_kernel(axes, owner_hbm, lengths_hbm, query_hbm, bias_ref, query_ref, owner, lengths, sems):
    small = [
        pltpu.make_async_copy(owner_hbm, owner, sems.at[0]),
        pltpu.make_async_copy(lengths_hbm, lengths, sems.at[1]),
    ]
    fetch = pltpu.make_async_copy(query_hbm, query_ref, sems.at[2])
    for copy in [*small, fetch]:
        copy.start()
    seq_len = bias_ref.shape[1]
    slot = lax.broadcasted_iota(jnp.int32, bias_ref.shape, 1)
    if axes:
        slot = slot + lax.rem(sum(lax.axis_index(axis) for axis in axes), 2) * (seq_len // 2)
        slot = jnp.where(slot >= seq_len, slot - seq_len, slot)
    for copy in small:
        copy.wait()
    bias_ref[...] = jnp.where(slot < lengths[owner[0]], 0.0, masked_score)
    fetch.wait()


def encode_kernel(packed, mine_ref, other_ref, gain_ref, cosine_ref, sine_ref, cache_ref):
    rank = gain_ref.shape[1]
    tokens, width = cosine_ref.shape
    projected = mine_ref[...] + other_ref[...]
    content = projected[:, :rank]
    mean = jnp.mean(content * content, axis=1, keepdims=True)
    normed = (content * lax.rsqrt(mean + 1e-06) * gain_ref[...]).astype(cache_ref.dtype)
    rotary = projected[:, rank:]
    swapped = jnp.concatenate([rotary[:, width // 2 :], rotary[:, : width // 2]], axis=1)
    rotated = rotary * cosine_ref[...] + swapped * sine_ref[...]
    if packed:
        for index in range(rank // lanes):
            cache_ref[index * tokens : (index + 1) * tokens, :] = normed[:, index * lanes : (index + 1) * lanes]
        paired_rows = jnp.concatenate([rotated[: tokens // 2], rotated[tokens // 2 :]], axis=1)
        cache_ref[rank // lanes * tokens :, :] = paired_rows.astype(cache_ref.dtype)
    else:
        cache_ref[:, :rank] = normed
        cache_ref[:, rank:] = rotated.astype(cache_ref.dtype)


def attend_kernel(packed, query_ref, bias_ref, *refs):
    count = 2 if packed else 1
    blocks, out_hbm, out, keys, sems = refs[:count], *refs[count:]
    rows, heads, rank = out_hbm.shape
    if packed:
        tokens = keys.shape[0] // 2
        width = keys.shape[1] - rank
        for half, block in enumerate(blocks):
            first = half * tokens
            for index in range(rank // lanes):
                keys[first : first + tokens, index * lanes : (index + 1) * lanes] = block[
                    index * tokens : (index + 1) * tokens, :
                ]
            paired_rows = block[rank // lanes * tokens :, :]
            keys[first : first + tokens // 2, rank:] = paired_rows[:, :width]
            keys[first + tokens // 2 : first + tokens, rank:] = paired_rows[:, width:]
    else:
        keys = blocks[0]
    query = query_ref[...].reshape(rows * heads, query_ref.shape[2])
    parts = sems.shape[0]
    per = rows // parts
    spans = [slice(part * per * heads, (part + 1) * per * heads) for part in range(parts)]
    products = [last_dims_dot(query[span], keys[...]) for span in spans]
    rounded, inverse = [], []
    for product in products:
        score = product * score_scale + bias_ref[...]
        weights = jnp.exp(score - jnp.max(score, axis=1, keepdims=True))
        inverse.append(1.0 / jnp.sum(weights, axis=1, keepdims=True))
        rounded.append(weights.astype(jnp.bfloat16))
    sums = [jnp.dot(part, keys[:, :rank], preferred_element_type=jnp.float32) for part in rounded]
    copies = []
    for part in range(parts):
        mine = pl.ds(part * per, per)
        out[mine] = (sums[part] * inverse[part]).astype(out.dtype).reshape(per, heads, rank)
        copy = pltpu.make_async_copy(out.at[mine], out_hbm.at[mine], sems.at[part])
        copy.start()
        copies.append(copy)
    for copy in copies:
        copy.wait()


def per_device(prompt_states, down_kv, kv_gain, queries, row_prompt, prompt_len):
    tokens, depth = prompt_states.shape
    latent = down_kv.shape[1]
    rank = kv_gain.shape[0]
    half = (latent - rank) // 2
    prompts = prompt_len.shape[0]
    pool = lax.axis_size("pool")
    seq_len = tokens * pool // prompts
    block = pool // prompts
    pool_at = lax.axis_index("pool")
    shift = row_prompt[0] ^ (pool_at // block)
    packed = block == 2 and lax.axis_size("tp") == 2 and rank % lanes == 0 and 4 * half == lanes and tokens % 32 == 0
    cache_shape = (tokens * latent // lanes, lanes) if packed else (tokens, latent)

    chunk = 512 if depth % 512 == 0 else depth
    edges = [0, *range(chunk // 2, depth, chunk), depth] if chunk < depth else [0, depth]
    spans = [(start, end - start) for start, end in zip(edges, edges[1:])]
    hbm = functools.partial(pltpu.with_memory_space_constraint, memory_space=pltpu.HBM)
    partial = pl.pallas_call(
        functools.partial(project_kernel, spans),
        out_shape=jax.ShapeDtypeStruct((tokens, latent), jnp.float32),
        in_specs=[in_hbm, in_hbm],
        out_specs=whole_vmem,
        scratch_shapes=[
            VMEM((tokens, depth), jnp.bfloat16),
            VMEM((latent, depth), jnp.bfloat16),
            pltpu.SemaphoreType.DMA,
            pltpu.SemaphoreType.DMA((len(spans),)),
        ],
        compiler_params=pltpu.CompilerParams(vmem_limit_bytes=16 * 2**20),
        cost_estimate=pl.CostEstimate(flops=2 * tokens * depth * latent, bytes_accessed=2 * depth * (latent + tokens), transcendentals=0),
        name="project",
    )(hbm(prompt_states), hbm(down_kv.T))
    cosine, sine = pl.pallas_call(
        functools.partial(angle_kernel, seq_len),
        out_shape=[jax.ShapeDtypeStruct((tokens, 2 * half), jnp.float32)] * 2,
        out_specs=[whole_vmem] * 2,
        compiler_params=pltpu.CompilerParams(vmem_limit_bytes=4 * 2**20),
        cost_estimate=pl.CostEstimate(flops=100 * tokens * half, bytes_accessed=4096, transcendentals=4 * tokens * half),
        name="angles",
    )()

    other = lax.ppermute(partial, "tp", [(0, 1), (1, 0)])
    cache = pl.pallas_call(
        functools.partial(encode_kernel, packed),
        out_shape=jax.ShapeDtypeStruct(cache_shape, jnp.bfloat16),
        in_specs=[whole_vmem] * 5,
        out_specs=whole_vmem,
        compiler_params=pltpu.CompilerParams(vmem_limit_bytes=4 * 2**20),
        name="encode",
    )(partial, other, kv_gain[None, :], cosine, sine)

    def mask(*axes):
        return pl.pallas_call(
            functools.partial(mask_kernel, axes),
            out_shape=[
                jax.ShapeDtypeStruct((1, seq_len), jnp.float32),
                pltpu.VMEM(queries.shape, queries.dtype),
            ],
            in_specs=[in_hbm] * 3,
            out_specs=[whole_vmem] * 2,
            scratch_shapes=[
                pltpu.SMEM(row_prompt.shape, jnp.int32),
                pltpu.SMEM(prompt_len.shape, jnp.int32),
                pltpu.SemaphoreType.DMA((3,)),
            ],
            compiler_params=pltpu.CompilerParams(vmem_limit_bytes=4 * 2**20),
            cost_estimate=pl.CostEstimate(flops=1000, bytes_accessed=4096, transcendentals=0),
            name="mask_and_queries",
        )(hbm(row_prompt), hbm(prompt_len), hbm(queries))

    def attend(ready, *blocks):
        bias, fetched = ready
        parts = 2 if queries.shape[0] % 2 == 0 else 1
        return pl.pallas_call(
            functools.partial(attend_kernel, len(blocks) > 1),
            out_shape=pltpu.HBM((queries.shape[0], queries.shape[1], rank), jnp.bfloat16),
            in_specs=[whole_vmem] * (2 + len(blocks)),
            out_specs=in_hbm,
            scratch_shapes=[
                VMEM((queries.shape[0], queries.shape[1], rank), jnp.bfloat16),
                VMEM((seq_len if len(blocks) > 1 else 16, latent), jnp.bfloat16),
                pltpu.SemaphoreType.DMA((parts,)),
            ],
            compiler_params=pltpu.CompilerParams(vmem_limit_bytes=(32 if seq_len > 1024 else 8) * 2**20),
            name="attend",
        )(fetched, bias, *blocks)

    def paired_step(step):
        pairs = [
            (at * 2 + c, ((at // 2 ^ step) * 2 + (at % 2 ^ c)) * 2 + c) for at in range(pool) for c in range(2)
        ]

        def run(rows):
            if step == 0:
                there = lax.ppermute(rows, "pool", [(at, at ^ 1) for at in range(pool)])
                return attend(mask("pool"), rows, there)
            here = lax.ppermute(rows, ("pool", "tp"), pairs)
            here, bias = lax.optimization_barrier((here, mask("pool", "tp")))
            return attend(bias, here, lax.ppermute(here, "tp", [(0, 1), (1, 0)]))

        return run

    if packed:
        return lax.switch(shift, [paired_step(step) for step in range(prompts)], cache)

    def fetch(step):
        pairs = [(at, at ^ (step * block)) for at in range(pool)]
        return lambda rows: lax.ppermute(rows, "pool", pairs) if step else rows

    here = lax.switch(shift, [fetch(step) for step in range(prompts)], cache)
    members = [list(range(b * block, (b + 1) * block)) for b in range(prompts)]
    return attend(mask(), lax.all_gather(here, "pool", axis=0, tiled=True, axis_index_groups=members))


def solution(mesh):
    placed = (
        P(("groups", "pool"), "tp"),
        P("tp", None),
        P(),
        P(("groups", "pool"), "tp", None),
        P(("groups", "pool")),
        P("groups"),
    )
    return jax.shard_map(
        per_device,
        mesh=mesh,
        in_specs=placed,
        out_specs=P(("groups", "pool"), "tp", None),
        check_vma=False,
    )
```
